256 devices in a mesh: dp: 4 (over z_lo, core), section: 4 (over x), et: 16 (over z_hi, y).
Axes of the slice: x: 4, y: 4, z: 8 (z_hi: 4, z_lo: 2; z = z_hi * 2 + z_lo), core: 2. Of those that a mesh axis runs over, the one named last changes fastest.
Arguments:
- handoff: bfloat16 [4, 8192, 3072], P('section', ('dp', 'et')), may hold values from -6 to 6
- fwd_slot: int32 [4, 8192], P('section', ('dp', 'et')), may hold values from -1 to 31, as said below
- fwd_weight: float32 [4, 8192], P('section', ('dp', 'et')), may hold values from 0.2 to 1
- stashed: bfloat16 [4, 8192, 3072], P('section', ('dp', 'et')), may hold values from -6 to 6
- back_slot: int32 [4, 8192], P('section', ('dp', 'et')), may hold values from -1 to 31, as said below
- back_weight: float32 [4, 8192], P('section', ('dp', 'et')), may hold values from 0.2 to 1
- grad_handoff: bfloat16 [4, 8192, 3072], P('section', ('dp', 'et')), may hold values from -6 to 6
- w_gate: bfloat16 [4, 3072, 5376], P('section', None, 'et'), may hold values from -0.109375 to 0.109375
- w_up: bfloat16 [4, 3072, 5376], P('section', None, 'et'), may hold values from -0.109375 to 0.109375
- w_down: bfloat16 [4, 5376, 3072], P('section', 'et'), may hold values from -0.078125 to 0.078125
Outputs:
- forward_out: bfloat16 [4, 8192, 3072], P('section', ('dp', 'et'))
- input_grad: bfloat16 [4, 8192, 3072], P('section', ('dp', 'et'))
- gate_grad: bfloat16 [4, 3072, 5376], P('section', 'dp', 'et')
- up_grad: bfloat16 [4, 3072, 5376], P('section', 'dp', 'et')
- down_grad: bfloat16 [4, 5376, 3072], P('section', 'et', 'dp')
The draws below stay inside these ranges and needn't reach their ends.
Inputs may be any that keep to these rules, and one draw needn't show every extreme that they name: `fwd_slot`: within each group of 128 rows of one device, the tokens routed to the expert carry the slots 0, 1, 2, ... in the order of the rows and the others carry -1; at least a quarter of 32 are routed; some device has exactly 32 routed tokens. `back_slot`: as for fwd_slot.
All inputs are finite; a program needn't handle non-finite values.
Results may differ from the reference program's by a relative error of at most 0.02.
Values may be sent and summed in bfloat16 or wider, within the bound.
No kernel may reach another device: no remote copies, remote signals or barrier semaphores. Data moves between devices by JAX's collectives and lax.ppermute only.
A program may use at most 128 MiB of HBM per device.

```python
import jax
import jax.numpy as jnp
from jax import lax

D = 3072
FF_WIN = 5376
TOK_DEV = 128
CAP = 32
TOKENS = 8192
SECTIONS = 4
N_DP = 4
N_ET = 16


def route_slots(key):
    blocks = TOKENS // TOK_DEV * SECTIONS
    key_order, key_count, key_full = jax.random.split(key, 3)
    scores = jax.random.randint(key_order, (blocks, TOK_DEV), 0, 2 ** 20)
    scores = scores * TOK_DEV + lax.broadcasted_iota(jnp.int32, (blocks, TOK_DEV), 1)
    ordering = jnp.argsort(jnp.argsort(scores, axis=1), axis=1).astype(jnp.int32)
    counts = jax.random.randint(key_count, (blocks,), CAP // 4, CAP + 1)
    fullest = jax.random.randint(key_full, (), 0, blocks)
    counts = jnp.where(jnp.arange(blocks) == fullest, CAP, counts)
    chosen = (ordering < counts[:, None]).astype(jnp.int32)
    slot_ids = jnp.where(chosen > 0, jnp.cumsum(chosen, axis=1) - 1, -1)
    return slot_ids.reshape(SECTIONS, TOKENS).astype(jnp.int32)


def draw_fwd_slot(key, part):
    key = jax.random.fold_in(key, 11)
    return route_slots(key)


def draw_back_slot(key, part):
    key = jax.random.fold_in(key, 23)
    return route_slots(key)


def level_of(stream_key, extent, shards, low, largest):
    def one(position, parts):
        steps = jax.random.uniform(jax.random.fold_in(jax.random.fold_in(stream_key, 6), position), (parts,), jnp.float32, low / len(shards), largest / len(shards))
        return jnp.repeat(jnp.exp(steps), extent[position] // parts).reshape((-1,) + (1,) * (len(extent) - position - 1))

    level = one(*shards[0])
    for cut in shards[1:]:
        level = level * one(*cut)
    return level


def normal_values(rng, shape, spread, reach, cuts=(), kind=jnp.bfloat16):
    array = spread * jax.random.normal(rng, shape, jnp.float32)
    if cuts:
        array = array * level_of(rng, shape, cuts, -0.22, 0.18)
    return jnp.clip(array, -reach, reach).astype(kind)


def setup_inputs(seed: int = 0) -> dict:
    keys = jax.random.split(jax.random.key(seed), 11)
    return {
        "handoff": normal_values(keys[0], (SECTIONS, TOKENS, D), 1.0, 6.0, ((0, 4), (1, 64))),
        "fwd_slot": draw_fwd_slot(jax.random.fold_in(keys[10], 71), 0),
        "fwd_weight": jnp.clip(0.2 + 0.8 * jax.random.uniform(keys[2], (SECTIONS, TOKENS), jnp.float32) ** level_of(keys[2], (SECTIONS, TOKENS), ((0, 4), (1, 64)), -0.2, 0.2), 0.2, 1.0),
        "stashed": normal_values(keys[3], (SECTIONS, TOKENS, D), 1.0, 6.0, ((0, 4), (1, 64))),
        "back_slot": draw_back_slot(jax.random.fold_in(keys[10], 71), 0),
        "back_weight": jnp.clip(0.2 + 0.8 * jax.random.uniform(keys[5], (SECTIONS, TOKENS), jnp.float32) ** level_of(keys[5], (SECTIONS, TOKENS), ((0, 4), (1, 64)), -0.2, 0.2), 0.2, 1.0),
        "grad_handoff": normal_values(keys[6], (SECTIONS, TOKENS, D), 1.0, 6.0, ((0, 4), (1, 64))),
        "w_gate": normal_values(keys[7], (SECTIONS, D, FF_WIN), D ** -0.5, 0.109375, ((0, 4), (2, 16))),
        "w_up": normal_values(keys[8], (SECTIONS, D, FF_WIN), D ** -0.5, 0.109375, ((0, 4), (2, 16))),
        "w_down": normal_values(keys[9], (SECTIONS, FF_WIN, D), FF_WIN ** -0.5, 0.078125, ((0, 4), (1, 16))),
    }


def rounded(value):
    return lax.optimization_barrier(value.astype(jnp.bfloat16)).astype(jnp.float32)


def pack_replica(row_block, slot_ids):
    sources = jnp.arange(N_ET * TOK_DEV, dtype=jnp.int32) // TOK_DEV
    target = jnp.where(slot_ids >= 0, sources * CAP + slot_ids, N_ET * CAP).astype(jnp.int32)
    packed = jnp.zeros((N_ET * CAP, row_block.shape[1]), row_block.dtype)
    return packed.at[target].set(row_block, mode="drop"), target


def unpack_replica(summed, target, slot_ids):
    picked = jnp.take(summed, jnp.minimum(target, N_ET * CAP - 1), axis=0)
    return jnp.where(slot_ids[:, None] >= 0, picked, jnp.zeros_like(picked))


def column_sum(make_term):
    share_cols = FF_WIN // N_ET
    summed = None
    for member in range(N_ET):
        partial_value = rounded(make_term(slice(member * share_cols, (member + 1) * share_cols)))
        summed = partial_value if summed is None else summed + partial_value
    return summed


def activations(packed, gate_w, up_w):
    pre_gate = jnp.dot(packed, gate_w, preferred_element_type=jnp.float32)
    pre_up = jnp.dot(packed, up_w, preferred_element_type=jnp.float32)
    sigmoid_gate = jax.nn.sigmoid(pre_gate)
    active = pre_gate * sigmoid_gate
    hidden = (active * pre_up).astype(jnp.bfloat16)
    return pre_gate, pre_up, sigmoid_gate, active, hidden


def reference(handoff, fwd_slot, fwd_weight, stashed, back_slot, back_weight, grad_handoff, w_gate, w_up, w_down):
    replica_rows = N_ET * TOK_DEV
    forward_list, input_list = [], []
    gate_list, up_list, down_list = [], [], []
    for section_id in range(SECTIONS):
        arrived = handoff[(section_id - 1) % SECTIONS]
        returned = grad_handoff[(section_id + 1) % SECTIONS]
        gate_w, up_w, down_w = w_gate[section_id], w_up[section_id], w_down[section_id]
        forward_rows, input_rows = [], []
        gate_acc = jnp.zeros((D, FF_WIN), jnp.float32)
        up_acc = jnp.zeros((D, FF_WIN), jnp.float32)
        down_acc = jnp.zeros((FF_WIN, D), jnp.float32)
        for replica in range(N_DP):
            first_row = replica * replica_rows
            last_row = first_row + replica_rows
            slot_ids = fwd_slot[section_id, first_row:last_row]
            packed, target = pack_replica(arrived[first_row:last_row], slot_ids)
            hidden = activations(packed, gate_w, up_w)[4]
            summed = column_sum(lambda columns: jnp.dot(hidden[:, columns], down_w[columns], preferred_element_type=jnp.float32))
            weights_row = fwd_weight[section_id, first_row:last_row]
            forward_rows.append((weights_row[:, None] * unpack_replica(summed, target, slot_ids)).astype(jnp.bfloat16))

            back_ids = back_slot[section_id, first_row:last_row]
            scaled = (back_weight[section_id, first_row:last_row][:, None] * returned[first_row:last_row].astype(jnp.float32)).astype(jnp.bfloat16)
            packed_grad, back_target = pack_replica(scaled, back_ids)
            packed_back, _ = pack_replica(stashed[section_id, first_row:last_row], back_ids)
            pre_gate, pre_up, sigmoid_gate, active, hidden = activations(packed_back, gate_w, up_w)
            grad_hidden = jnp.dot(packed_grad, down_w.T, preferred_element_type=jnp.float32)
            grad_upact = (grad_hidden * active).astype(jnp.bfloat16)
            grad_gateact = (grad_hidden * pre_up * sigmoid_gate * (1.0 + pre_gate * (1.0 - sigmoid_gate))).astype(jnp.bfloat16)
            gate_acc = gate_acc + rounded(jnp.dot(packed_back.T, grad_gateact, preferred_element_type=jnp.float32))
            up_acc = up_acc + rounded(jnp.dot(packed_back.T, grad_upact, preferred_element_type=jnp.float32))
            down_acc = down_acc + rounded(jnp.dot(hidden.T, packed_grad, preferred_element_type=jnp.float32))
            grad_packed = column_sum(lambda columns: jnp.dot(grad_gateact[:, columns], gate_w[:, columns].T, preferred_element_type=jnp.float32) + jnp.dot(grad_upact[:, columns], up_w[:, columns].T, preferred_element_type=jnp.float32))
            input_rows.append(unpack_replica(grad_packed, back_target, back_ids).astype(jnp.bfloat16))
        forward_list.append(jnp.concatenate(forward_rows, axis=0))
        input_list.append(jnp.concatenate(input_rows, axis=0))
        gate_list.append(gate_acc.astype(jnp.bfloat16))
        up_list.append(up_acc.astype(jnp.bfloat16))
        down_list.append(down_acc.astype(jnp.bfloat16))
    return (jnp.stack(forward_list), jnp.stack(input_list), jnp.stack(gate_list), jnp.stack(up_list), jnp.stack(down_list))
```

```python
import jax
import jax.numpy as jnp
from jax import lax
from jax.sharding import PartitionSpec as P

CAP = 32
SIDE = 4
F32 = jnp.float32
BF16 = jnp.bfloat16
CONTRACT_LAST = (((1,), (1,)), ((), ()))
CONTRACT_FIRST = (((0,), (0,)), ((), ()))


def passed_along(block, axis, distance):
    devices = range(lax.axis_size(axis))
    route = [((i - distance) % len(devices), i) for i in devices]
    return lax.ppermute(block, axis, route)


def fetched(block, dz, dy):
    route = []
    for z in range(SIDE):
        for y in range(SIDE):
            source = (z + dz) % SIDE * SIDE + (y + dy) % SIDE
            route.append((source, z * SIDE + y))
    return lax.ppermute(block, "et", route)


def swapped(block, bit):
    return lax.ppermute(block, "dp", [(i ^ bit, i) for i in range(4)])


def gather_z(block):
    above = fetched(block, 1, 0)
    below = fetched(block, -1, 0)
    far = fetched(block, 2, 0)
    return jnp.concatenate([block, above, far, below], axis=0)


def gather_y(rows):
    half = rows.shape[0] // 2
    right = fetched(rows, 0, 1)
    left = fetched(rows, 0, -1)
    far_first = fetched(right[:half], 0, 1)
    far_last = fetched(left[half:], 0, -1)
    return jnp.concatenate([rows, right, far_first, far_last, left], axis=0)


def scatter_y(terms):
    count = terms.shape[0] // SIDE
    half = count // 2
    own, right, far, left = (terms[i * count : (i + 1) * count] for i in range(SIDE))
    for_right = fetched(far[:half], 0, -1)
    for_left = fetched(far[half:], 0, 1)
    right = jnp.concatenate([added(right[:half], for_right), right[half:]], axis=0)
    left = jnp.concatenate([left[:half], added(left[half:], for_left)], axis=0)
    from_left = fetched(right, 0, -1)
    from_right = fetched(left, 0, 1)
    return added(own, from_left, from_right)


def scatter_z(terms):
    own, above, far, below = (terms[i * CAP : (i + 1) * CAP] for i in range(SIDE))
    parts = (fetched(above, -1, 0), fetched(far, 2, 0), fetched(below, 1, 0))
    return own.astype(F32) + parts[0].astype(F32) + parts[1].astype(F32) + parts[2].astype(F32)


def added(*terms):
    total = terms[0].astype(F32)
    for term in terms[1:]:
        total = total + term.astype(F32)
    return total.astype(BF16)


def summed_over_dp(terms, axis):
    place = lax.axis_index("dp")
    core, z_lo = place % 2, place // 2
    size = terms.shape[axis] // 4

    def piece(z, c):
        return lax.dynamic_slice_in_dim(terms, (z * 2 + c) * size, size, axis)

    other = jnp.stack([piece(0, 1 - core), piece(1, 1 - core)])
    came = swapped(other, 1)
    keep = piece(z_lo, core).astype(F32) + lax.dynamic_index_in_dim(came, z_lo, 0, False).astype(F32)
    give = piece(1 - z_lo, core).astype(F32) + lax.dynamic_index_in_dim(
        came, 1 - z_lo, 0, False
    ).astype(F32)
    return (keep + swapped(give.astype(BF16), 2).astype(F32)).astype(BF16)


def pack_rows(row_block, slot_ids):
    places = lax.broadcasted_iota(jnp.int32, (CAP, slot_ids.shape[0]), 0)
    picker = (places == slot_ids[None, :]).astype(BF16)
    return jnp.dot(picker, row_block, preferred_element_type=F32).astype(BF16)


def unpack_rows(packed, slot_ids):
    places = lax.broadcasted_iota(jnp.int32, (slot_ids.shape[0], CAP), 1)
    picker = (places == slot_ids[:, None]).astype(F32)
    return jnp.dot(picker, packed, precision=lax.Precision.HIGHEST, preferred_element_type=F32)


def activations(row_block, gate_w, up_w):
    pre_gate = jnp.dot(row_block, gate_w, preferred_element_type=F32)
    pre_up = jnp.dot(row_block, up_w, preferred_element_type=F32)
    sigmoid_gate = jax.nn.sigmoid(pre_gate)
    active = pre_gate * sigmoid_gate
    hidden = (active * pre_up).astype(BF16)
    return (pre_gate, pre_up, sigmoid_gate, active, hidden)


def per_device(
    handoff,
    fwd_slot,
    fwd_weight,
    stashed,
    back_slot,
    back_weight,
    grad_handoff,
    w_gate,
    w_up,
    w_down,
):
    gate_w, up_w, down_w = (w_gate[0], w_up[0], w_down[0])
    fwd_ids = fwd_slot[0]
    back_ids = back_slot[0]
    returned = passed_along(grad_handoff, "section", -1)[0]
    arrived = passed_along(handoff, "section", 1)[0]

    back_rows = gather_y(gather_z(pack_rows(stashed[0], back_ids)))
    scaled = (back_weight[0][:, None] * returned.astype(F32)).astype(BF16)
    grad_rows = gather_y(gather_z(pack_rows(scaled, back_ids)))
    fwd_rows = gather_y(gather_z(pack_rows(arrived, fwd_ids)))

    pre_gate, pre_up, sigmoid_gate, active, hidden = activations(back_rows, gate_w, up_w)
    grad_hidden = lax.dot_general(grad_rows, down_w, CONTRACT_LAST, preferred_element_type=F32)
    grad_upact = (grad_hidden * active).astype(BF16)
    grad_gateact = (
        grad_hidden * pre_up * sigmoid_gate * (1.0 + pre_gate * (1.0 - sigmoid_gate))
    ).astype(BF16)
    from_gate = lax.dot_general(grad_gateact, gate_w, CONTRACT_LAST, preferred_element_type=F32)
    from_up = lax.dot_general(grad_upact, up_w, CONTRACT_LAST, preferred_element_type=F32)
    input_sum = scatter_z(scatter_y((from_gate + from_up).astype(BF16)))
    input_grad = unpack_rows(input_sum, back_ids).astype(BF16)

    gate_term = lax.dot_general(back_rows, grad_gateact, CONTRACT_FIRST, preferred_element_type=F32)
    up_term = lax.dot_general(back_rows, grad_upact, CONTRACT_FIRST, preferred_element_type=F32)
    down_term = lax.dot_general(hidden, grad_rows, CONTRACT_FIRST, preferred_element_type=F32)
    gate_sum = summed_over_dp(gate_term.astype(BF16), 0)
    up_sum = summed_over_dp(up_term.astype(BF16), 0)
    down_sum = summed_over_dp(down_term.astype(BF16), 1)

    fwd_hidden = activations(fwd_rows, gate_w, up_w)[4]
    fwd_sum = scatter_z(scatter_y(jnp.dot(fwd_hidden, down_w, preferred_element_type=F32).astype(BF16)))
    forward_out = (fwd_weight[0][:, None] * unpack_rows(fwd_sum, fwd_ids)).astype(BF16)
    return (forward_out[None], input_grad[None], gate_sum[None], up_sum[None], down_sum[None])


def solution(mesh):
    placed = (
        P("section", ("dp", "et"), None),
        P("section", ("dp", "et")),
        P("section", ("dp", "et")),
        P("section", ("dp", "et"), None),
        P("section", ("dp", "et")),
        P("section", ("dp", "et")),
        P("section", ("dp", "et"), None),
        P("section", None, "et"),
        P("section", None, "et"),
        P("section", "et", None),
    )
    return jax.shard_map(
        per_device,
        mesh=mesh,
        in_specs=placed,
        out_specs=(
            P("section", ("dp", "et"), None),
            P("section", ("dp", "et"), None),
            P("section", "dp", "et"),
            P("section", "dp", "et"),
            P("section", "et", "dp"),
        ),
        check_vma=False,
    )
```

```python
import jax
import jax.numpy as jnp
from jax import lax
from jax.experimental import pallas as pl
from jax.experimental.pallas import tpu as pltpu
from jax.sharding import PartitionSpec as P

CAP = 32
SIDE = 4
F32 = jnp.float32
BF16 = jnp.bfloat16
CONTRACT_LAST = (((1,), (1,)), ((), ()))
CONTRACT_FIRST = (((0,), (0,)), ((), ()))


def passed_along(block, axis, distance):
    devices = range(lax.axis_size(axis))
    route = [((i - distance) % len(devices), i) for i in devices]
    return lax.ppermute(block, axis, route)


def fetched(block, dz, dy):
    route = []
    for z in range(SIDE):
        for y in range(SIDE):
            source = (z + dz) % SIDE * SIDE + (y + dy) % SIDE
            route.append((source, z * SIDE + y))
    return lax.ppermute(block, "et", route)


def swapped(block, bit):
    return lax.ppermute(block, "dp", [(i ^ bit, i) for i in range(4)])


def tied(value, *others):
    return lax.optimization_barrier((value,) + others)[0]


def exchanged_z(blocks):
    groups = [[z * SIDE + y for z in range(SIDE)] for y in range(SIDE)]
    return lax.all_to_all(blocks, "et", 0, 0, axis_index_groups=groups, tiled=True)


def gathered_z(block):
    return exchanged_z(jnp.concatenate([block] * SIDE, axis=0))


def summed_z(terms):
    return sum(part.astype(F32) for part in split(exchanged_z(terms)))


def fetched_z(block):
    return (fetched(block, 1, 0), fetched(block, 2, 0), fetched(block, -1, 0))


def z_place(dz):
    z = lax.axis_index("et") // SIDE
    return (z + dz) % SIDE * CAP


def z_ordered(own, came):
    rows = jnp.zeros((SIDE * CAP, own.shape[1]), own.dtype)
    for dz, part in enumerate((own,) + came):
        rows = lax.dynamic_update_slice_in_dim(rows, part, z_place(dz), 0)
    return rows


def sent_z(terms):
    own, above, far, below = (
        lax.dynamic_slice_in_dim(terms, z_place(dz), CAP, 0) for dz in range(SIDE)
    )
    return own, (fetched(above, -1, 0), fetched(far, 2, 0), fetched(below, 1, 0))


def total_of(own, came):
    total = own.astype(F32)
    for term in came:
        total = total + term.astype(F32)
    return total


def y_first(rows):
    return (fetched(rows, 0, 1), fetched(rows, 0, -1))


def y_second(right, left):
    half = right.shape[0] // 2
    return (fetched(right[:half], 0, 1), fetched(left[half:], 0, -1))


def pieces(rows, near, far):
    return (rows, near[0], far[0], far[1], near[1])


def split(terms):
    count = terms.shape[0] // SIDE
    return [terms[i * count : (i + 1) * count] for i in range(SIDE)]


def far_out(first, last):
    return (fetched(first, 0, -1), fetched(last, 0, 1))


def near_out(right, left, came):
    half = right.shape[0] // 2
    right = jnp.concatenate([added(right[:half], came[0]), right[half:]], axis=0)
    left = jnp.concatenate([left[:half], added(left[half:], came[1])], axis=0)
    return (fetched(right, 0, -1), fetched(left, 0, 1))


def added(*terms):
    total = terms[0].astype(F32)
    for term in terms[1:]:
        total = total + term.astype(F32)
    return total.astype(BF16)


def pack_rows(row_block, slot_ids):
    places = lax.broadcasted_iota(jnp.int32, (CAP, slot_ids.shape[0]), 0)
    picker = (places == slot_ids[None, :]).astype(BF16)
    return jnp.dot(picker, row_block, preferred_element_type=F32).astype(BF16)


def unpack_rows(packed, slot_ids):
    places = lax.broadcasted_iota(jnp.int32, (slot_ids.shape[0], CAP), 1)
    picker = (places == slot_ids[:, None]).astype(F32)
    return jnp.dot(picker, packed, precision=lax.Precision.HIGHEST, preferred_element_type=F32)


def kernel_call(body, outs, places, scratch, *operands):
    return pl.pallas_call(
        body,
        out_shape=outs,
        in_specs=[pl.BlockSpec(memory_space=place) for place in places],
        out_specs=[pl.BlockSpec(memory_space=pltpu.VMEM)] * len(outs),
        scratch_shapes=scratch,
        compiler_params=pltpu.CompilerParams(vmem_limit_bytes=60 * 2**20),
        cost_estimate=pl.CostEstimate(flops=1000, bytes_accessed=1000, transcendentals=0),
    )(*operands)


def shape_of(*shape, kind=BF16):
    return jax.ShapeDtypeStruct(shape, kind)


def started(sources, targets, sems, first=0):
    copies = []
    for i, (source, target) in enumerate(zip(sources, targets)):
        copies.append(pltpu.make_async_copy(source, target, sems.at[first + i]))
        copies[-1].start()
    return copies


def pieces_of(rows):
    count = rows.shape[0] // SIDE
    sizes = (count, count, count // 2, count // 2, count)
    at, views = 0, []
    for size in sizes:
        views.append(rows.at[pl.ds(at, size)])
        at += size
    return views


def gate_and_up(rows, gate, up):
    pre_gate = lax.dot_general(rows, gate, CONTRACT_LAST, preferred_element_type=F32)
    pre_up = lax.dot_general(rows, up, CONTRACT_LAST, preferred_element_type=F32)
    sigmoid_gate = jax.nn.sigmoid(pre_gate)
    return pre_gate, pre_up, sigmoid_gate, pre_gate * sigmoid_gate


def act_body(*refs):
    parts, (gate, up), (hidden, active, slope), (rows, gate_v, up_v, sems) = (
        refs[:5], refs[5:7], refs[7:10], refs[10:]
    )
    weights = started((gate, up), (gate_v, up_v), sems)
    copies = started(parts, pieces_of(rows), sems, 2)
    for copy in weights:
        copy.wait()
    half = rows.shape[0] // 2
    for i, needed in enumerate((copies[:2], copies[2:])):
        for copy in needed:
            copy.wait()
        here = pl.ds(i * half, half)
        pre_gate, pre_up, sigmoid_gate, act = gate_and_up(rows[here, :], gate_v[...], up_v[...])
        hidden[here, :] = (act * pre_up).astype(BF16)
        active[here, :] = act
        slope[here, :] = pre_up * sigmoid_gate * (1.0 + pre_gate * (1.0 - sigmoid_gate))


def act_call(parts, gate_w, up_w):
    units, width = gate_w.shape
    total = SIDE * parts[0].shape[0]
    return kernel_call(
        act_body,
        (shape_of(total, units), shape_of(total, units, kind=F32), shape_of(total, units, kind=F32)),
        [pl.ANY] * 7,
        [
            pltpu.VMEM((total, width), BF16),
            pltpu.VMEM((units, width), BF16),
            pltpu.VMEM((units, width), BF16),
            pltpu.SemaphoreType.DMA((7,)),
        ],
        *parts, gate_w, up_w,
    )


def spread(i, columns, terms, outs):
    own, right, far_first, far_last, left = outs
    count = own.shape[0]
    if i == 0:
        own[:, columns] = terms[:count]
        right[:, columns] = terms[count:]
    else:
        far_first[:, columns] = terms[: count // 2]
        far_last[:, columns] = terms[count // 2 : count]
        left[:, columns] = terms[count:]


def term_shapes(count, width):
    return tuple(shape_of(n, width) for n in (count, count, count // 2, count // 2, count))


def grad_body(*refs):
    parts, (active, slope), (gate, up, down) = refs[:5], refs[5:7], refs[7:10]
    (gate_act, up_act), outs = refs[10:12], refs[12:17]
    rows, gate_v, up_v, down_v, sems = refs[17:]
    first = started((down,), (down_v,), sems)
    copies = started(parts, pieces_of(rows), sems, 1)
    later = started((gate, up), (gate_v, up_v), sems, 6)
    first[0].wait()
    half, width = rows.shape[0] // 2, rows.shape[1]
    step = width // SIDE
    for i, needed in enumerate((copies[:2], copies[2:])):
        for copy in needed:
            copy.wait()
        here = pl.ds(i * half, half)
        grad_hidden = lax.dot_general(
            rows[here, :], down_v[...], CONTRACT_LAST, preferred_element_type=F32
        )
        up_now = (grad_hidden * active[here, :]).astype(BF16)
        gate_now = (grad_hidden * slope[here, :]).astype(BF16)
        up_act[here, :] = up_now
        gate_act[here, :] = gate_now
        if i == 0:
            for copy in later:
                copy.wait()
        for j in range(SIDE):
            columns = pl.ds(j * step, step)
            terms = jnp.dot(gate_now, gate_v[:, columns], preferred_element_type=F32) + jnp.dot(
                up_now, up_v[:, columns], preferred_element_type=F32
            )
            spread(i, columns, terms.astype(BF16), outs)


def grad_call(parts, active, slope, gate_w, up_w, down_w):
    units, width = gate_w.shape
    count = parts[0].shape[0]
    total = SIDE * count
    return kernel_call(
        grad_body,
        (shape_of(total, units), shape_of(total, units)) + term_shapes(count, width),
        [pl.ANY] * 5 + [pltpu.VMEM] * 2 + [pl.ANY] * 3,
        [
            pltpu.VMEM((total, width), BF16),
            pltpu.VMEM((units, width), BF16),
            pltpu.VMEM((units, width), BF16),
            pltpu.VMEM((units, width), BF16),
            pltpu.SemaphoreType.DMA((8,)),
        ],
        *parts, active, slope, gate_w, up_w, down_w,
    )


def sums_body(*refs):
    stash, grads, (gate_act, up_act, hidden, order) = refs[:5], refs[5:10], refs[10:14]
    (keep, send), (stash_v, grad_v, sems) = refs[14:16], refs[16:]
    copies = started(stash, pieces_of(stash_v), sems) + started(grads, pieces_of(grad_v), sems, 5)
    units, size = gate_act.shape[1], keep.shape[2]
    for copy in copies:
        copy.wait()
    lefts = ((gate_act[...], stash_v), (up_act[...], stash_v), (hidden[...], grad_v))
    for i, out in ((1, send), (0, keep)):
        for j in range(2):
            columns = pl.ds(pl.multiple_of(order[2 * i + j] * size, 128), size)
            for k, (lhs, rhs) in enumerate(lefts):
                out[j, pl.ds(k * units, units), :] = lax.dot_general(
                    lhs, rhs[:, columns], CONTRACT_FIRST, preferred_element_type=F32
                ).astype(BF16)


def sums_call(stash, grads, gate_act, up_act, hidden, order):
    total, units = gate_act.shape
    width = stash[0].shape[1]
    out = shape_of(2, 3 * units, width // 4)
    return kernel_call(
        sums_body,
        (out, out),
        [pl.ANY] * 10 + [pltpu.VMEM] * 3 + [pltpu.SMEM],
        [
            pltpu.VMEM((total, width), BF16),
            pltpu.VMEM((total, width), BF16),
            pltpu.SemaphoreType.DMA((10,)),
        ],
        *stash, *grads, gate_act, up_act, hidden, order,
    )


def fwd_body(*refs):
    parts, (gate, up, down), outs = refs[:5], refs[5:8], refs[8:13]
    rows, gate_v, up_v, down_v, sems = refs[13:]
    weights = started((gate, up), (gate_v, up_v), sems)
    copies = started(parts, pieces_of(rows), sems, 2)
    later = started((down,), (down_v,), sems, 7)
    for copy in weights:
        copy.wait()
    half, width = rows.shape[0] // 2, rows.shape[1]
    step = width // SIDE
    for i, needed in enumerate((copies[:2], copies[2:])):
        for copy in needed:
            copy.wait()
        _, pre_up, _, act = gate_and_up(rows[pl.ds(i * half, half), :], gate_v[...], up_v[...])
        hidden = (act * pre_up).astype(BF16)
        if i == 0:
            later[0].wait()
        for j in range(SIDE):
            columns = pl.ds(j * step, step)
            terms = jnp.dot(hidden, down_v[:, columns], preferred_element_type=F32)
            spread(i, columns, terms.astype(BF16), outs)


def fwd_call(parts, gate_w, up_w, down_w):
    units, width = gate_w.shape
    count = parts[0].shape[0]
    return kernel_call(
        fwd_body,
        term_shapes(count, width),
        [pl.ANY] * 8,
        [
            pltpu.VMEM((SIDE * count, width), BF16),
            pltpu.VMEM((units, width), BF16),
            pltpu.VMEM((units, width), BF16),
            pltpu.VMEM((units, width), BF16),
            pltpu.SemaphoreType.DMA((8,)),
        ],
        *parts, gate_w, up_w, down_w,
    )


def per_device(
    handoff,
    fwd_slot,
    fwd_weight,
    stashed,
    back_slot,
    back_weight,
    grad_handoff,
    w_gate,
    w_up,
    w_down,
):
    gate_w, up_w, down_w = (w_gate[0].T, w_up[0].T, w_down[0])
    fwd_ids = fwd_slot[0]
    back_ids = back_slot[0]
    place = lax.axis_index("dp")
    core, z_lo = place % 2, place // 2

    returned = passed_along(grad_handoff, "section", -1)[0]
    arrived = passed_along(handoff, "section", 1)[0]

    stash_own = pack_rows(stashed[0], back_ids)
    stash_rows = z_ordered(stash_own, fetched_z(stash_own))
    stash_near = y_first(stash_rows)
    returned = tied(returned, stash_rows)
    scaled = (back_weight[0][:, None] * returned.astype(F32)).astype(BF16)
    grad_own = pack_rows(scaled, back_ids)
    grad_rows = z_ordered(grad_own, fetched_z(tied(grad_own, stash_rows)))
    grad_near = y_first(tied(grad_rows, *stash_near))
    fwd_own = pack_rows(tied(arrived, grad_own), fwd_ids)
    stash_far = y_second(*stash_near)
    fwd_rows = gathered_z(tied(fwd_own, grad_rows, *stash_far))
    grad_far = y_second(*(tied(t, *stash_far) for t in grad_near))
    fwd_near = y_first(tied(fwd_rows, *grad_near))
    back_all = pieces(tied(stash_rows, fwd_rows, *grad_near), stash_near, stash_far)
    hidden, active, slope = act_call(back_all, gate_w, up_w)
    grad_all = pieces(tied(grad_rows, active), grad_near, grad_far)
    gate_act, up_act, own, right, far_a, far_b, left = grad_call(
        grad_all, active, slope, gate_w, up_w, down_w
    )
    input_far = far_out(far_a, far_b)
    fwd_far = y_second(*(tied(t, far_a) for t in fwd_near))
    order = jnp.stack(
        [(z_lo ^ i) * 2 + (core ^ j) for j in range(2) for i in range(2)]
    ).astype(jnp.int32)
    keep, send = sums_call(
        back_all, grad_all, gate_act, up_act, hidden, order
    )
    came = swapped(send, 1)
    give = added(keep[1], came[1])
    input_near = near_out(right, left, tuple(tied(t, *fwd_far) for t in input_far))
    cut = give.shape[0] // 3 * 2
    gave = (swapped(give[:cut], 2), swapped(give[cut:], 2))
    fwd_terms = fwd_call(
        pieces(tied(fwd_rows, give, *input_far), fwd_near, fwd_far), gate_w, up_w, down_w
    )
    fwd_out_far = far_out(fwd_terms[2], fwd_terms[3])
    input_terms = added(own, *input_near)
    fwd_out_near = near_out(
        fwd_terms[1], fwd_terms[4], tuple(tied(t, input_terms, gave[0]) for t in fwd_out_far)
    )
    input_came = exchanged_z(input_terms)
    fwd_z = added(fwd_terms[0], *fwd_out_near)
    input_sum = sum(part.astype(F32) for part in split(tied(input_came, fwd_z)))
    input_grad = unpack_rows(input_sum, back_ids).astype(BF16)
    near_sums = added(tied(keep[0][:cut], fwd_z), came[0][:cut], gave[0])
    gate_sum, up_sum = near_sums[: cut // 2].T, near_sums[cut // 2 :].T
    down_sum = added(tied(keep[0][cut:], fwd_z), came[0][cut:], gave[1])
    fwd_sum = total_of(*sent_z(fwd_z))
    forward_out = (fwd_weight[0][:, None] * unpack_rows(fwd_sum, fwd_ids)).astype(BF16)
    return (forward_out[None], input_grad[None], gate_sum[None], up_sum[None], down_sum[None])


def solution(mesh):
    placed = (
        P("section", ("dp", "et"), None),
        P("section", ("dp", "et")),
        P("section", ("dp", "et")),
        P("section", ("dp", "et"), None),
        P("section", ("dp", "et")),
        P("section", ("dp", "et")),
        P("section", ("dp", "et"), None),
        P("section", None, "et"),
        P("section", None, "et"),
        P("section", "et", None),
    )
    return jax.shard_map(
        per_device,
        mesh=mesh,
        in_specs=placed,
        out_specs=(
            P("section", ("dp", "et"), None),
            P("section", ("dp", "et"), None),
            P("section", "dp", "et"),
            P("section", "dp", "et"),
            P("section", "et", "dp"),
        ),
        check_vma=False,
    )
```

```python
import jax
import jax.numpy as jnp
from jax import lax
from jax.experimental import pallas as pl
from jax.experimental.pallas import tpu as pltpu
from jax.sharding import PartitionSpec as P

CAP = 32
SIDE = 4
F32 = jnp.float32
BF16 = jnp.bfloat16
CONTRACT_LAST = (((1,), (1,)), ((), ()))
CONTRACT_FIRST = (((0,), (0,)), ((), ()))


def passed_along(block, axis, distance):
    devices = range(lax.axis_size(axis))
    route = [((i - distance) % len(devices), i) for i in devices]
    return lax.ppermute(block, axis, route)


def fetched(block, dz, dy):
    route = []
    for z in range(SIDE):
        for y in range(SIDE):
            source = (z + dz) % SIDE * SIDE + (y + dy) % SIDE
            route.append((source, z * SIDE + y))
    return lax.ppermute(block, "et", route)


def swapped(block, bit):
    return lax.ppermute(block, "dp", [(i ^ bit, i) for i in range(4)])


def tied(value, *others):
    return lax.optimization_barrier((value,) + others)[0]


def exchanged_z(blocks):
    groups = [[z * SIDE + y for z in range(SIDE)] for y in range(SIDE)]
    return lax.all_to_all(blocks, "et", 0, 0, axis_index_groups=groups, tiled=True)


def gathered_z(block):
    return exchanged_z(jnp.concatenate([block] * SIDE, axis=0))


def summed_z(terms):
    return sum(part.astype(F32) for part in split(exchanged_z(terms)))


def fetched_z(block):
    return (fetched(block, 1, 0), fetched(block, 2, 0), fetched(block, -1, 0))


def z_place(dz):
    z = lax.axis_index("et") // SIDE
    return (z + dz) % SIDE * CAP


def z_ordered(own, came):
    rows = jnp.zeros((SIDE * CAP, own.shape[1]), own.dtype)
    for dz, part in enumerate((own,) + came):
        rows = lax.dynamic_update_slice_in_dim(rows, part, z_place(dz), 0)
    return rows


def sent_z(terms):
    own, above, far, below = (
        lax.dynamic_slice_in_dim(terms, z_place(dz), CAP, 0) for dz in range(SIDE)
    )
    return own, (fetched(above, -1, 0), fetched(far, 2, 0), fetched(below, 1, 0))


def total_of(own, came):
    total = own.astype(F32)
    for term in came:
        total = total + term.astype(F32)
    return total


def y_first(rows):
    return (fetched(rows, 0, 1), fetched(rows, 0, -1))


def y_second(right, left):
    half = right.shape[0] // 2
    return (fetched(right[:half], 0, 1), fetched(left[half:], 0, -1))


def pieces(rows, near, far):
    return (rows, near[0], far[0], far[1], near[1])


def split(terms):
    count = terms.shape[0] // SIDE
    return [terms[i * count : (i + 1) * count] for i in range(SIDE)]


def far_out(first, last):
    return (fetched(first, 0, -1), fetched(last, 0, 1))


def near_out(right, left, came):
    half = right.shape[0] // 2
    right = jnp.concatenate([added(right[:half], came[0]), right[half:]], axis=0)
    left = jnp.concatenate([left[:half], added(left[half:], came[1])], axis=0)
    return (fetched(right, 0, -1), fetched(left, 0, 1))


def added(*terms):
    total = terms[0].astype(F32)
    for term in terms[1:]:
        total = total + term.astype(F32)
    return total.astype(BF16)


def pack_rows(row_block, slot_ids):
    places = lax.broadcasted_iota(jnp.int32, (CAP, slot_ids.shape[0]), 0)
    picker = (places == slot_ids[None, :]).astype(BF16)
    return jnp.dot(picker, row_block, preferred_element_type=F32).astype(BF16)


def unpack_rows(packed, slot_ids):
    places = lax.broadcasted_iota(jnp.int32, (slot_ids.shape[0], CAP), 1)
    picker = (places == slot_ids[:, None]).astype(F32)
    return jnp.dot(picker, packed, precision=lax.Precision.HIGHEST, preferred_element_type=F32)


def kernel_call(body, outs, places, scratch, *operands):
    return pl.pallas_call(
        body,
        out_shape=outs,
        in_specs=[pl.BlockSpec(memory_space=place) for place in places],
        out_specs=[pl.BlockSpec(memory_space=pltpu.VMEM)] * len(outs),
        scratch_shapes=scratch,
        compiler_params=pltpu.CompilerParams(vmem_limit_bytes=60 * 2**20),
        cost_estimate=pl.CostEstimate(flops=1000, bytes_accessed=1000, transcendentals=0),
    )(*operands)


def shape_of(*shape, kind=BF16):
    return jax.ShapeDtypeStruct(shape, kind)


def started(sources, targets, sems, first=0):
    copies = []
    for i, (source, target) in enumerate(zip(sources, targets)):
        copies.append(pltpu.make_async_copy(source, target, sems.at[first + i]))
        copies[-1].start()
    return copies


def pieces_of(rows):
    count = rows.shape[0] // SIDE
    sizes = (count, count, count // 2, count // 2, count)
    at, views = 0, []
    for size in sizes:
        views.append(rows.at[pl.ds(at, size)])
        at += size
    return views


def gate_and_up(rows, gate, up):
    pre_gate = lax.dot_general(rows, gate, CONTRACT_LAST, preferred_element_type=F32)
    pre_up = lax.dot_general(rows, up, CONTRACT_LAST, preferred_element_type=F32)
    sigmoid_gate = jax.nn.sigmoid(pre_gate)
    return pre_gate, pre_up, sigmoid_gate, pre_gate * sigmoid_gate


def act_body(*refs):
    parts, (gate, up), (hidden, active, slope), (rows, gate_v, up_v, sems) = (
        refs[:5], refs[5:7], refs[7:10], refs[10:]
    )
    weights = started((gate, up), (gate_v, up_v), sems)
    copies = started(parts, pieces_of(rows), sems, 2)
    for copy in weights:
        copy.wait()
    half = rows.shape[0] // 2
    for i, needed in enumerate((copies[:2], copies[2:])):
        for copy in needed:
            copy.wait()
        here = pl.ds(i * half, half)
        pre_gate, pre_up, sigmoid_gate, act = gate_and_up(rows[here, :], gate_v[...], up_v[...])
        hidden[here, :] = (act * pre_up).astype(BF16)
        active[here, :] = act
        slope[here, :] = pre_up * sigmoid_gate * (1.0 + pre_gate * (1.0 - sigmoid_gate))


def act_call(parts, gate_w, up_w):
    units, width = gate_w.shape
    total = SIDE * parts[0].shape[0]
    return kernel_call(
        act_body,
        (shape_of(total, units), shape_of(total, units, kind=F32), shape_of(total, units, kind=F32)),
        [pl.ANY] * 7,
        [
            pltpu.VMEM((total, width), BF16),
            pltpu.VMEM((units, width), BF16),
            pltpu.VMEM((units, width), BF16),
            pltpu.SemaphoreType.DMA((7,)),
        ],
        *parts, gate_w, up_w,
    )


def spread(i, columns, terms, outs):
    own, right, far_first, far_last, left = outs
    count = own.shape[0]
    if i == 0:
        own[:, columns] = terms[:count]
        right[:, columns] = terms[count:]
    else:
        far_first[:, columns] = terms[: count // 2]
        far_last[:, columns] = terms[count // 2 : count]
        left[:, columns] = terms[count:]


def term_shapes(count, width):
    return tuple(shape_of(n, width) for n in (count, count, count // 2, count // 2, count))


def grad_body(*refs):
    parts, (active, slope), (gate, up, down) = refs[:5], refs[5:7], refs[7:10]
    (gate_act, up_act), outs = refs[10:12], refs[12:17]
    rows, gate_v, up_v, down_v, sems = refs[17:]
    first = started((down,), (down_v,), sems)
    copies = started(parts, pieces_of(rows), sems, 1)
    later = started((gate, up), (gate_v, up_v), sems, 6)
    first[0].wait()
    half, width = rows.shape[0] // 2, rows.shape[1]
    step = width // SIDE
    for i, needed in enumerate((copies[:2], copies[2:])):
        for copy in needed:
            copy.wait()
        here = pl.ds(i * half, half)
        grad_hidden = lax.dot_general(
            rows[here, :], down_v[...], CONTRACT_LAST, preferred_element_type=F32
        )
        up_now = (grad_hidden * active[here, :]).astype(BF16)
        gate_now = (grad_hidden * slope[here, :]).astype(BF16)
        up_act[here, :] = up_now
        gate_act[here, :] = gate_now
        if i == 0:
            for copy in later:
                copy.wait()
        for j in range(SIDE):
            columns = pl.ds(j * step, step)
            terms = jnp.dot(gate_now, gate_v[:, columns], preferred_element_type=F32) + jnp.dot(
                up_now, up_v[:, columns], preferred_element_type=F32
            )
            spread(i, columns, terms.astype(BF16), outs)


def grad_call(parts, active, slope, gate_w, up_w, down_w):
    units, width = gate_w.shape
    count = parts[0].shape[0]
    total = SIDE * count
    return kernel_call(
        grad_body,
        (shape_of(total, units), shape_of(total, units)) + term_shapes(count, width),
        [pl.ANY] * 5 + [pltpu.VMEM] * 2 + [pl.ANY] * 3,
        [
            pltpu.VMEM((total, width), BF16),
            pltpu.VMEM((units, width), BF16),
            pltpu.VMEM((units, width), BF16),
            pltpu.VMEM((units, width), BF16),
            pltpu.SemaphoreType.DMA((8,)),
        ],
        *parts, active, slope, gate_w, up_w, down_w,
    )


def sums_body(*refs):
    stash, grads, (gate_act, up_act, hidden, order) = refs[:5], refs[5:10], refs[10:14]
    (keep, send), (stash_v, grad_v, sems) = refs[14:16], refs[16:]
    copies = started(stash, pieces_of(stash_v), sems) + started(grads, pieces_of(grad_v), sems, 5)
    units, size = gate_act.shape[1], keep.shape[2]
    for copy in copies:
        copy.wait()
    lefts = ((gate_act[...], stash_v), (up_act[...], stash_v), (hidden[...], grad_v))
    for i, out in ((1, send), (0, keep)):
        for j in range(2):
            columns = pl.ds(pl.multiple_of(order[2 * i + j] * size, 128), size)
            for k, (lhs, rhs) in enumerate(lefts):
                out[j, pl.ds(k * units, units), :] = lax.dot_general(
                    lhs, rhs[:, columns], CONTRACT_FIRST, preferred_element_type=F32
                ).astype(BF16)


def sums_call(stash, grads, gate_act, up_act, hidden, order):
    total, units = gate_act.shape
    width = stash[0].shape[1]
    out = shape_of(2, 3 * units, width // 4)
    return kernel_call(
        sums_body,
        (out, out),
        [pl.ANY] * 10 + [pltpu.VMEM] * 3 + [pltpu.SMEM],
        [
            pltpu.VMEM((total, width), BF16),
            pltpu.VMEM((total, width), BF16),
            pltpu.SemaphoreType.DMA((10,)),
        ],
        *stash, *grads, gate_act, up_act, hidden, order,
    )


def fwd_body(*refs):
    parts, (gate, up, down), outs = refs[:5], refs[5:8], refs[8:13]
    rows, gate_v, up_v, down_v, sems = refs[13:]
    weights = started((gate, up), (gate_v, up_v), sems)
    copies = started(parts, pieces_of(rows), sems, 2)
    later = started((down,), (down_v,), sems, 7)
    for copy in weights:
        copy.wait()
    half, width = rows.shape[0] // 2, rows.shape[1]
    step = width // SIDE
    for i, needed in enumerate((copies[:2], copies[2:])):
        for copy in needed:
            copy.wait()
        _, pre_up, _, act = gate_and_up(rows[pl.ds(i * half, half), :], gate_v[...], up_v[...])
        hidden = (act * pre_up).astype(BF16)
        if i == 0:
            later[0].wait()
        for j in range(SIDE):
            columns = pl.ds(j * step, step)
            terms = jnp.dot(hidden, down_v[:, columns], preferred_element_type=F32)
            spread(i, columns, terms.astype(BF16), outs)


def fwd_call(parts, gate_w, up_w, down_w):
    units, width = gate_w.shape
    count = parts[0].shape[0]
    return kernel_call(
        fwd_body,
        term_shapes(count, width),
        [pl.ANY] * 8,
        [
            pltpu.VMEM((SIDE * count, width), BF16),
            pltpu.VMEM((units, width), BF16),
            pltpu.VMEM((units, width), BF16),
            pltpu.VMEM((units, width), BF16),
            pltpu.SemaphoreType.DMA((8,)),
        ],
        *parts, gate_w, up_w, down_w,
    )


def per_device(
    handoff,
    fwd_slot,
    fwd_weight,
    stashed,
    back_slot,
    back_weight,
    grad_handoff,
    w_gate,
    w_up,
    w_down,
):
    gate_w, up_w, down_w = (w_gate[0].T, w_up[0].T, w_down[0])
    fwd_ids = fwd_slot[0]
    back_ids = back_slot[0]
    place = lax.axis_index("dp")
    core, z_lo = place % 2, place // 2

    returned = passed_along(grad_handoff, "section", -1)[0]
    arrived = passed_along(handoff, "section", 1)[0]

    stash_own = pack_rows(stashed[0], back_ids)
    stash_rows = z_ordered(stash_own, fetched_z(stash_own))
    stash_near = y_first(stash_rows)
    returned = tied(returned, stash_rows)
    scaled = (back_weight[0][:, None] * returned.astype(F32)).astype(BF16)
    grad_own = pack_rows(scaled, back_ids)
    grad_rows = z_ordered(grad_own, fetched_z(tied(grad_own, stash_rows)))
    grad_near = y_first(tied(grad_rows, *stash_near))
    fwd_own = pack_rows(tied(arrived, grad_own), fwd_ids)
    stash_far = y_second(*stash_near)
    fwd_rows = gathered_z(tied(fwd_own, grad_rows, *stash_far))
    back_all = pieces(tied(stash_rows, grad_rows), stash_near, stash_far)
    hidden, active, slope = act_call(back_all, gate_w, up_w)
    grad_far = y_second(*(tied(t, hidden) for t in grad_near))
    fwd_near = y_first(tied(fwd_rows, *grad_far))
    grad_all = pieces(tied(grad_rows, active, fwd_rows), grad_near, grad_far)
    gate_act, up_act, own, right, far_a, far_b, left = grad_call(
        grad_all, active, slope, gate_w, up_w, down_w
    )
    input_far = far_out(far_a, far_b)
    fwd_far = y_second(*(tied(t, far_a) for t in fwd_near))
    order = jnp.stack(
        [(z_lo ^ i) * 2 + (core ^ j) for j in range(2) for i in range(2)]
    ).astype(jnp.int32)
    keep, send = sums_call(
        back_all, grad_all, gate_act, up_act, hidden, order
    )
    came = swapped(tied(send, *fwd_near), 1)
    give = added(keep[1], came[1])
    input_near = near_out(right, left, tuple(tied(t, give, *fwd_far) for t in input_far))
    gave = swapped(give, 2)
    fwd_terms = fwd_call(
        pieces(tied(fwd_rows, give), fwd_near, fwd_far), gate_w, up_w, down_w
    )
    fwd_out_far = far_out(fwd_terms[2], fwd_terms[3])
    input_terms = added(own, *input_near)
    fwd_out_near = near_out(
        fwd_terms[1], fwd_terms[4], tuple(tied(t, input_terms, gave) for t in fwd_out_far)
    )
    input_came = exchanged_z(input_terms)
    fwd_z = added(fwd_terms[0], *fwd_out_near)
    input_sum = sum(part.astype(F32) for part in split(tied(input_came, fwd_z)))
    input_grad = unpack_rows(input_sum, back_ids).astype(BF16)
    sums = added(tied(keep[0], fwd_z), came[0], gave)
    third = sums.shape[0] // 3
    gate_sum, up_sum, down_sum = sums[:third].T, sums[third : 2 * third].T, sums[2 * third :]
    fwd_sum = total_of(*sent_z(fwd_z))
    forward_out = (fwd_weight[0][:, None] * unpack_rows(fwd_sum, fwd_ids)).astype(BF16)
    return (forward_out[None], input_grad[None], gate_sum[None], up_sum[None], down_sum[None])


def solution(mesh):
    placed = (
        P("section", ("dp", "et"), None),
        P("section", ("dp", "et")),
        P("section", ("dp", "et")),
        P("section", ("dp", "et"), None),
        P("section", ("dp", "et")),
        P("section", ("dp", "et")),
        P("section", ("dp", "et"), None),
        P("section", None, "et"),
        P("section", None, "et"),
        P("section", "et", None),
    )
    return jax.shard_map(
        per_device,
        mesh=mesh,
        in_specs=placed,
        out_specs=(
            P("section", ("dp", "et"), None),
            P("section", ("dp", "et"), None),
            P("section", "dp", "et"),
            P("section", "dp", "et"),
            P("section", "et", "dp"),
        ),
        check_vma=False,
    )
```

```python
import jax
import jax.numpy as jnp
from jax import lax
from jax.experimental import pallas as pl
from jax.experimental.pallas import tpu as pltpu
from jax.sharding import PartitionSpec as P

CAP = 32
SIDE = 4
F32 = jnp.float32
BF16 = jnp.bfloat16
CONTRACT_LAST = (((1,), (1,)), ((), ()))
CONTRACT_FIRST = (((0,), (0,)), ((), ()))


def passed_along(block, axis, distance):
    devices = range(lax.axis_size(axis))
    route = [((i - distance) % len(devices), i) for i in devices]
    return lax.ppermute(block, axis, route)


def fetched(block, dz, dy):
    route = []
    for z in range(SIDE):
        for y in range(SIDE):
            source = (z + dz) % SIDE * SIDE + (y + dy) % SIDE
            route.append((source, z * SIDE + y))
    return lax.ppermute(block, "et", route)


def swapped(block, bit):
    return lax.ppermute(block, "dp", [(i ^ bit, i) for i in range(4)])


def tied(value, *others):
    return lax.optimization_barrier((value,) + others)[0]


def exchanged_z(blocks):
    groups = [[z * SIDE + y for z in range(SIDE)] for y in range(SIDE)]
    return lax.all_to_all(blocks, "et", 0, 0, axis_index_groups=groups, tiled=True)


def gathered_z(block):
    return exchanged_z(jnp.concatenate([block] * SIDE, axis=0))


def summed_z(terms):
    return sum(part.astype(F32) for part in split(exchanged_z(terms)))


def fetched_z(block):
    return (fetched(block, 1, 0), fetched(block, 2, 0), fetched(block, -1, 0))


def z_place(dz):
    z = lax.axis_index("et") // SIDE
    return (z + dz) % SIDE * CAP


def z_ordered(own, came):
    rows = jnp.zeros((SIDE * CAP, own.shape[1]), own.dtype)
    for dz, part in enumerate((own,) + came):
        rows = lax.dynamic_update_slice_in_dim(rows, part, z_place(dz), 0)
    return rows


def sent_z(terms):
    own, above, far, below = (
        lax.dynamic_slice_in_dim(terms, z_place(dz), CAP, 0) for dz in range(SIDE)
    )
    return own, (fetched(above, -1, 0), fetched(far, 2, 0), fetched(below, 1, 0))


def total_of(own, came):
    total = own.astype(F32)
    for term in came:
        total = total + term.astype(F32)
    return total


def y_first(rows):
    return (fetched(rows, 0, 1), fetched(rows, 0, -1))


def y_second(right, left):
    half = right.shape[0] // 2
    return (fetched(right[:half], 0, 1), fetched(left[half:], 0, -1))


def pieces(rows, near, far):
    return (rows, near[0], far[0], far[1], near[1])


def split(terms):
    count = terms.shape[0] // SIDE
    return [terms[i * count : (i + 1) * count] for i in range(SIDE)]


def far_out(first, last):
    return (fetched(first, 0, -1), fetched(last, 0, 1))


def near_out(right, left, came):
    half = right.shape[0] // 2
    right = jnp.concatenate([added(right[:half], came[0]), right[half:]], axis=0)
    left = jnp.concatenate([left[:half], added(left[half:], came[1])], axis=0)
    return (fetched(right, 0, -1), fetched(left, 0, 1))


def added(*terms):
    total = terms[0].astype(F32)
    for term in terms[1:]:
        total = total + term.astype(F32)
    return total.astype(BF16)


def pack_rows(row_block, slot_ids):
    places = lax.broadcasted_iota(jnp.int32, (CAP, slot_ids.shape[0]), 0)
    picker = (places == slot_ids[None, :]).astype(BF16)
    return jnp.dot(picker, row_block, preferred_element_type=F32).astype(BF16)


def unpack_rows(packed, slot_ids):
    places = lax.broadcasted_iota(jnp.int32, (slot_ids.shape[0], CAP), 1)
    picker = (places == slot_ids[:, None]).astype(F32)
    return jnp.dot(picker, packed, precision=lax.Precision.HIGHEST, preferred_element_type=F32)


def kernel_call(body, outs, places, scratch, *operands):
    return pl.pallas_call(
        body,
        out_shape=outs,
        in_specs=[pl.BlockSpec(memory_space=place) for place in places],
        out_specs=[pl.BlockSpec(memory_space=pltpu.VMEM)] * len(outs),
        scratch_shapes=scratch,
        compiler_params=pltpu.CompilerParams(vmem_limit_bytes=60 * 2**20),
        cost_estimate=pl.CostEstimate(flops=1000, bytes_accessed=1000, transcendentals=0),
    )(*operands)


def shape_of(*shape, kind=BF16):
    return jax.ShapeDtypeStruct(shape, kind)


def started(sources, targets, sems, first=0):
    copies = []
    for i, (source, target) in enumerate(zip(sources, targets)):
        copies.append(pltpu.make_async_copy(source, target, sems.at[first + i]))
        copies[-1].start()
    return copies


def pieces_of(rows):
    count = rows.shape[0] // SIDE
    sizes = (count, count, count // 2, count // 2, count)
    at, views = 0, []
    for size in sizes:
        views.append(rows.at[pl.ds(at, size)])
        at += size
    return views


def gate_and_up(rows, gate, up):
    pre_gate = lax.dot_general(rows, gate, CONTRACT_LAST, preferred_element_type=F32)
    pre_up = lax.dot_general(rows, up, CONTRACT_LAST, preferred_element_type=F32)
    sigmoid_gate = jax.nn.sigmoid(pre_gate)
    return pre_gate, pre_up, sigmoid_gate, pre_gate * sigmoid_gate


def act_body(*refs):
    parts, (gate, up), (hidden, active, slope), (rows, gate_v, up_v, sems) = (
        refs[:5], refs[5:7], refs[7:10], refs[10:]
    )
    weights = started((gate, up), (gate_v, up_v), sems)
    copies = started(parts, pieces_of(rows), sems, 2)
    for copy in weights:
        copy.wait()
    half = rows.shape[0] // 2
    for i, needed in enumerate((copies[:2], copies[2:])):
        for copy in needed:
            copy.wait()
        here = pl.ds(i * half, half)
        pre_gate, pre_up, sigmoid_gate, act = gate_and_up(rows[here, :], gate_v[...], up_v[...])
        hidden[here, :] = (act * pre_up).astype(BF16)
        active[here, :] = act
        slope[here, :] = pre_up * sigmoid_gate * (1.0 + pre_gate * (1.0 - sigmoid_gate))


def act_call(parts, gate_w, up_w):
    units, width = gate_w.shape
    total = SIDE * parts[0].shape[0]
    return kernel_call(
        act_body,
        (shape_of(total, units), shape_of(total, units, kind=F32), shape_of(total, units, kind=F32)),
        [pl.ANY] * 7,
        [
            pltpu.VMEM((total, width), BF16),
            pltpu.VMEM((units, width), BF16),
            pltpu.VMEM((units, width), BF16),
            pltpu.SemaphoreType.DMA((7,)),
        ],
        *parts, gate_w, up_w,
    )


def spread(i, columns, terms, outs):
    own, right, far_first, far_last, left = outs
    count = own.shape[0]
    if i == 0:
        own[:, columns] = terms[:count]
        right[:, columns] = terms[count:]
    else:
        far_first[:, columns] = terms[: count // 2]
        far_last[:, columns] = terms[count // 2 : count]
        left[:, columns] = terms[count:]


def term_shapes(count, width):
    return tuple(shape_of(n, width) for n in (count, count, count // 2, count // 2, count))


def grad_body(*refs):
    parts, (active, slope), (gate, up, down) = refs[:5], refs[5:7], refs[7:10]
    (gate_act, up_act), outs = refs[10:12], refs[12:17]
    rows, gate_v, up_v, down_v, sems = refs[17:]
    first = started((down,), (down_v,), sems)
    copies = started(parts, pieces_of(rows), sems, 1)
    later = started((gate, up), (gate_v, up_v), sems, 6)
    first[0].wait()
    half, width = rows.shape[0] // 2, rows.shape[1]
    step = width // SIDE
    for i, needed in enumerate((copies[:2], copies[2:])):
        for copy in needed:
            copy.wait()
        here = pl.ds(i * half, half)
        grad_hidden = lax.dot_general(
            rows[here, :], down_v[...], CONTRACT_LAST, preferred_element_type=F32
        )
        up_now = (grad_hidden * active[here, :]).astype(BF16)
        gate_now = (grad_hidden * slope[here, :]).astype(BF16)
        up_act[here, :] = up_now
        gate_act[here, :] = gate_now
        if i == 0:
            for copy in later:
                copy.wait()
        for j in range(SIDE):
            columns = pl.ds(j * step, step)
            terms = jnp.dot(gate_now, gate_v[:, columns], preferred_element_type=F32) + jnp.dot(
                up_now, up_v[:, columns], preferred_element_type=F32
            )
            spread(i, columns, terms.astype(BF16), outs)


def grad_call(parts, active, slope, gate_w, up_w, down_w):
    units, width = gate_w.shape
    count = parts[0].shape[0]
    total = SIDE * count
    return kernel_call(
        grad_body,
        (shape_of(total, units), shape_of(total, units)) + term_shapes(count, width),
        [pl.ANY] * 5 + [pltpu.VMEM] * 2 + [pl.ANY] * 3,
        [
            pltpu.VMEM((total, width), BF16),
            pltpu.VMEM((units, width), BF16),
            pltpu.VMEM((units, width), BF16),
            pltpu.VMEM((units, width), BF16),
            pltpu.SemaphoreType.DMA((8,)),
        ],
        *parts, active, slope, gate_w, up_w, down_w,
    )


def sums_body(*refs):
    stash, grads, (gate_act, up_act, hidden, order) = refs[:5], refs[5:10], refs[10:14]
    (keep, send), (stash_v, grad_v, sems) = refs[14:16], refs[16:]
    copies = started(stash, pieces_of(stash_v), sems) + started(grads, pieces_of(grad_v), sems, 5)
    units, size = gate_act.shape[1], keep.shape[2]
    for copy in copies:
        copy.wait()
    lefts = ((gate_act[...], stash_v), (up_act[...], stash_v), (hidden[...], grad_v))
    for i, out in ((1, send), (0, keep)):
        for j in range(2):
            columns = pl.ds(pl.multiple_of(order[2 * i + j] * size, 128), size)
            for k, (lhs, rhs) in enumerate(lefts):
                out[j, pl.ds(k * units, units), :] = lax.dot_general(
                    lhs, rhs[:, columns], CONTRACT_FIRST, preferred_element_type=F32
                ).astype(BF16)


def sums_call(stash, grads, gate_act, up_act, hidden, order):
    total, units = gate_act.shape
    width = stash[0].shape[1]
    out = shape_of(2, 3 * units, width // 4)
    return kernel_call(
        sums_body,
        (out, out),
        [pl.ANY] * 10 + [pltpu.VMEM] * 3 + [pltpu.SMEM],
        [
            pltpu.VMEM((total, width), BF16),
            pltpu.VMEM((total, width), BF16),
            pltpu.SemaphoreType.DMA((10,)),
        ],
        *stash, *grads, gate_act, up_act, hidden, order,
    )


def fwd_body(*refs):
    parts, (gate, up, down), outs = refs[:5], refs[5:8], refs[8:13]
    rows, gate_v, up_v, down_v, sems = refs[13:]
    weights = started((gate, up), (gate_v, up_v), sems)
    copies = started(parts, pieces_of(rows), sems, 2)
    later = started((down,), (down_v,), sems, 7)
    for copy in weights:
        copy.wait()
    half, width = rows.shape[0] // 2, rows.shape[1]
    step = width // SIDE
    for i, needed in enumerate((copies[:2], copies[2:])):
        for copy in needed:
            copy.wait()
        _, pre_up, _, act = gate_and_up(rows[pl.ds(i * half, half), :], gate_v[...], up_v[...])
        hidden = (act * pre_up).astype(BF16)
        if i == 0:
            later[0].wait()
        for j in range(SIDE):
            columns = pl.ds(j * step, step)
            terms = jnp.dot(hidden, down_v[:, columns], preferred_element_type=F32)
            spread(i, columns, terms.astype(BF16), outs)


def fwd_call(parts, gate_w, up_w, down_w):
    units, width = gate_w.shape
    count = parts[0].shape[0]
    return kernel_call(
        fwd_body,
        term_shapes(count, width),
        [pl.ANY] * 8,
        [
            pltpu.VMEM((SIDE * count, width), BF16),
            pltpu.VMEM((units, width), BF16),
            pltpu.VMEM((units, width), BF16),
            pltpu.VMEM((units, width), BF16),
            pltpu.SemaphoreType.DMA((8,)),
        ],
        *parts, gate_w, up_w, down_w,
    )


def per_device(
    handoff,
    fwd_slot,
    fwd_weight,
    stashed,
    back_slot,
    back_weight,
    grad_handoff,
    w_gate,
    w_up,
    w_down,
):
    gate_w, up_w, down_w = (w_gate[0].T, w_up[0].T, w_down[0])
    fwd_ids = fwd_slot[0]
    back_ids = back_slot[0]
    place = lax.axis_index("dp")
    core, z_lo = place % 2, place // 2

    returned = passed_along(grad_handoff, "section", -1)[0]
    arrived = passed_along(handoff, "section", 1)[0]

    stash_own = pack_rows(stashed[0], back_ids)
    stash_rows = z_ordered(stash_own, fetched_z(stash_own))
    stash_near = y_first(stash_rows)
    returned = tied(returned, stash_rows)
    scaled = (back_weight[0][:, None] * returned.astype(F32)).astype(BF16)
    grad_own = pack_rows(scaled, back_ids)
    grad_rows = z_ordered(grad_own, fetched_z(tied(grad_own, stash_rows)))
    grad_near = y_first(tied(grad_rows, *stash_near))
    fwd_own = pack_rows(tied(arrived, grad_own), fwd_ids)
    stash_far = y_second(*stash_near)
    fwd_rows = gathered_z(tied(fwd_own, grad_rows, *stash_far))
    back_all = pieces(tied(stash_rows, grad_rows), stash_near, stash_far)
    hidden, active, slope = act_call(back_all, gate_w, up_w)
    grad_far = y_second(*(tied(t, hidden) for t in grad_near))
    fwd_near = y_first(tied(fwd_rows, *grad_far))
    grad_all = pieces(tied(grad_rows, active, fwd_rows), grad_near, grad_far)
    gate_act, up_act, own, right, far_a, far_b, left = grad_call(
        grad_all, active, slope, gate_w, up_w, down_w
    )
    input_far = far_out(far_a, far_b)
    fwd_far = y_second(*(tied(t, far_a) for t in fwd_near))
    order = jnp.stack(
        [(z_lo ^ i) * 2 + (core ^ j) for j in range(2) for i in range(2)]
    ).astype(jnp.int32)
    keep, send = sums_call(
        back_all, grad_all, gate_act, up_act, hidden, order
    )
    came = swapped(tied(send, *fwd_near, *input_far), 1)
    give = added(keep[1], came[1])
    input_near = near_out(right, left, tuple(tied(t, give, *fwd_far) for t in input_far))
    gave = swapped(give, 2)
    fwd_terms = fwd_call(
        pieces(tied(fwd_rows, give), fwd_near, fwd_far), gate_w, up_w, down_w
    )
    fwd_out_far = far_out(fwd_terms[2], fwd_terms[3])
    input_terms = added(own, *input_near)
    fwd_out_near = near_out(
        fwd_terms[1], fwd_terms[4], tuple(tied(t, input_terms, gave) for t in fwd_out_far)
    )
    input_came = exchanged_z(input_terms)
    fwd_z = added(fwd_terms[0], *fwd_out_near)
    input_sum = sum(part.astype(F32) for part in split(tied(input_came, fwd_z)))
    input_grad = unpack_rows(input_sum, back_ids).astype(BF16)
    sums = added(tied(keep[0], fwd_z), came[0], gave)
    third = sums.shape[0] // 3
    gate_sum, up_sum, down_sum = sums[:third].T, sums[third : 2 * third].T, sums[2 * third :]
    fwd_sum = total_of(*sent_z(fwd_z))
    forward_out = (fwd_weight[0][:, None] * unpack_rows(fwd_sum, fwd_ids)).astype(BF16)
    return (forward_out[None], input_grad[None], gate_sum[None], up_sum[None], down_sum[None])


def solution(mesh):
    placed = (
        P("section", ("dp", "et"), None),
        P("section", ("dp", "et")),
        P("section", ("dp", "et")),
        P("section", ("dp", "et"), None),
        P("section", ("dp", "et")),
        P("section", ("dp", "et")),
        P("section", ("dp", "et"), None),
        P("section", None, "et"),
        P("section", None, "et"),
        P("section", "et", None),
    )
    return jax.shard_map(
        per_device,
        mesh=mesh,
        in_specs=placed,
        out_specs=(
            P("section", ("dp", "et"), None),
            P("section", ("dp", "et"), None),
            P("section", "dp", "et"),
            P("section", "dp", "et"),
            P("section", "et", "dp"),
        ),
        check_vma=False,
    )
```

```python
import jax
import jax.numpy as jnp
from jax import lax
from jax.experimental import pallas as pl
from jax.experimental.pallas import tpu as pltpu
from jax.sharding import PartitionSpec as P

CAP = 32
SIDE = 4
F32 = jnp.float32
BF16 = jnp.bfloat16
CONTRACT_LAST = (((1,), (1,)), ((), ()))
CONTRACT_FIRST = (((0,), (0,)), ((), ()))


def passed_along(block, axis, distance):
    devices = range(lax.axis_size(axis))
    route = [((i - distance) % len(devices), i) for i in devices]
    return lax.ppermute(block, axis, route)


def fetched(block, dz, dy):
    route = []
    for z in range(SIDE):
        for y in range(SIDE):
            source = (z + dz) % SIDE * SIDE + (y + dy) % SIDE
            route.append((source, z * SIDE + y))
    return lax.ppermute(block, "et", route)


def swapped(block, bit):
    return lax.ppermute(block, "dp", [(i ^ bit, i) for i in range(4)])


def tied(value, *others):
    return lax.optimization_barrier((value,) + others)[0]


def exchanged_z(blocks):
    groups = [[z * SIDE + y for z in range(SIDE)] for y in range(SIDE)]
    return lax.all_to_all(blocks, "et", 0, 0, axis_index_groups=groups, tiled=True)


def gathered_z(block):
    return exchanged_z(jnp.concatenate([block] * SIDE, axis=0))


def summed_z(terms):
    return sum(part.astype(F32) for part in split(exchanged_z(terms)))


def fetched_z(block):
    return (fetched(block, 1, 0), fetched(block, 2, 0), fetched(block, -1, 0))


def z_place(dz):
    z = lax.axis_index("et") // SIDE
    return (z + dz) % SIDE * CAP


def z_ordered(own, came):
    rows = jnp.zeros((SIDE * CAP, own.shape[1]), own.dtype)
    for dz, part in enumerate((own,) + came):
        rows = lax.dynamic_update_slice_in_dim(rows, part, z_place(dz), 0)
    return rows


def sent_z(terms):
    own, above, far, below = (
        lax.dynamic_slice_in_dim(terms, z_place(dz), CAP, 0) for dz in range(SIDE)
    )
    return own, (fetched(above, -1, 0), fetched(far, 2, 0), fetched(below, 1, 0))


def total_of(own, came):
    total = own.astype(F32)
    for term in came:
        total = total + term.astype(F32)
    return total


def y_first(rows):
    return (fetched(rows, 0, 1), fetched(rows, 0, -1))


def y_second(right, left):
    half = right.shape[0] // 2
    return (fetched(right[:half], 0, 1), fetched(left[half:], 0, -1))


def pieces(rows, near, far):
    return (rows, near[0], far[0], far[1], near[1])


def split(terms):
    count = terms.shape[0] // SIDE
    return [terms[i * count : (i + 1) * count] for i in range(SIDE)]


def far_out(first, last):
    return (fetched(first, 0, -1), fetched(last, 0, 1))


def near_out(right, left, came):
    half = right.shape[0] // 2
    right = jnp.concatenate([added(right[:half], came[0]), right[half:]], axis=0)
    left = jnp.concatenate([left[:half], added(left[half:], came[1])], axis=0)
    return (fetched(right, 0, -1), fetched(left, 0, 1))


def added(*terms):
    total = terms[0].astype(F32)
    for term in terms[1:]:
        total = total + term.astype(F32)
    return total.astype(BF16)


def pack_rows(row_block, slot_ids):
    places = lax.broadcasted_iota(jnp.int32, (CAP, slot_ids.shape[0]), 0)
    picker = (places == slot_ids[None, :]).astype(BF16)
    return jnp.dot(picker, row_block, preferred_element_type=F32).astype(BF16)


def unpack_rows(packed, slot_ids):
    places = lax.broadcasted_iota(jnp.int32, (slot_ids.shape[0], CAP), 1)
    picker = (places == slot_ids[:, None]).astype(F32)
    return jnp.dot(picker, packed, precision=lax.Precision.HIGHEST, preferred_element_type=F32)


def kernel_call(body, outs, places, scratch, *operands):
    return pl.pallas_call(
        body,
        out_shape=outs,
        in_specs=[pl.BlockSpec(memory_space=place) for place in places],
        out_specs=[pl.BlockSpec(memory_space=pltpu.VMEM)] * len(outs),
        scratch_shapes=scratch,
        compiler_params=pltpu.CompilerParams(vmem_limit_bytes=60 * 2**20),
        cost_estimate=pl.CostEstimate(flops=1000, bytes_accessed=1000, transcendentals=0),
    )(*operands)


def shape_of(*shape, kind=BF16):
    return jax.ShapeDtypeStruct(shape, kind)


def started(sources, targets, sems, first=0):
    copies = []
    for i, (source, target) in enumerate(zip(sources, targets)):
        copies.append(pltpu.make_async_copy(source, target, sems.at[first + i]))
        copies[-1].start()
    return copies


def pieces_of(rows):
    count = rows.shape[0] // SIDE
    sizes = (count, count, count // 2, count // 2, count)
    at, views = 0, []
    for size in sizes:
        views.append(rows.at[pl.ds(at, size)])
        at += size
    return views


def gate_and_up(rows, gate, up):
    pre_gate = lax.dot_general(rows, gate, CONTRACT_LAST, preferred_element_type=F32)
    pre_up = lax.dot_general(rows, up, CONTRACT_LAST, preferred_element_type=F32)
    sigmoid_gate = jax.nn.sigmoid(pre_gate)
    return pre_gate, pre_up, sigmoid_gate, pre_gate * sigmoid_gate


def act_body(*refs):
    parts, (gate, up), (hidden, active, slope), (rows, gate_v, up_v, sems) = (
        refs[:5], refs[5:7], refs[7:10], refs[10:]
    )
    weights = started((gate, up), (gate_v, up_v), sems)
    copies = started(parts, pieces_of(rows), sems, 2)
    for copy in weights:
        copy.wait()
    half = rows.shape[0] // 2
    for i, needed in enumerate((copies[:2], copies[2:])):
        for copy in needed:
            copy.wait()
        here = pl.ds(i * half, half)
        pre_gate, pre_up, sigmoid_gate, act = gate_and_up(rows[here, :], gate_v[...], up_v[...])
        hidden[here, :] = (act * pre_up).astype(BF16)
        active[here, :] = act
        slope[here, :] = pre_up * sigmoid_gate * (1.0 + pre_gate * (1.0 - sigmoid_gate))


def act_call(parts, gate_w, up_w):
    units, width = gate_w.shape
    total = SIDE * parts[0].shape[0]
    return kernel_call(
        act_body,
        (shape_of(total, units), shape_of(total, units, kind=F32), shape_of(total, units, kind=F32)),
        [pl.ANY] * 7,
        [
            pltpu.VMEM((total, width), BF16),
            pltpu.VMEM((units, width), BF16),
            pltpu.VMEM((units, width), BF16),
            pltpu.SemaphoreType.DMA((7,)),
        ],
        *parts, gate_w, up_w,
    )


def spread(i, columns, terms, outs):
    own, right, far_first, far_last, left = outs
    count = own.shape[0]
    if i == 0:
        own[:, columns] = terms[:count]
        right[:, columns] = terms[count:]
    else:
        far_first[:, columns] = terms[: count // 2]
        far_last[:, columns] = terms[count // 2 : count]
        left[:, columns] = terms[count:]


def term_shapes(count, width):
    return tuple(shape_of(n, width) for n in (count, count, count // 2, count // 2, count))


def grad_body(*refs):
    parts, (active, slope), (gate, up, down) = refs[:5], refs[5:7], refs[7:10]
    (gate_act, up_act), outs = refs[10:12], refs[12:17]
    rows, gate_v, up_v, down_v, sems = refs[17:]
    first = started((down,), (down_v,), sems)
    copies = started(parts, pieces_of(rows), sems, 1)
    later = started((gate, up), (gate_v, up_v), sems, 6)
    first[0].wait()
    half, width = rows.shape[0] // 2, rows.shape[1]
    step = width // SIDE
    for i, needed in enumerate((copies[:2], copies[2:])):
        for copy in needed:
            copy.wait()
        here = pl.ds(i * half, half)
        grad_hidden = lax.dot_general(
            rows[here, :], down_v[...], CONTRACT_LAST, preferred_element_type=F32
        )
        up_now = (grad_hidden * active[here, :]).astype(BF16)
        gate_now = (grad_hidden * slope[here, :]).astype(BF16)
        up_act[here, :] = up_now
        gate_act[here, :] = gate_now
        if i == 0:
            for copy in later:
                copy.wait()
        for j in range(SIDE):
            columns = pl.ds(j * step, step)
            terms = jnp.dot(gate_now, gate_v[:, columns], preferred_element_type=F32) + jnp.dot(
                up_now, up_v[:, columns], preferred_element_type=F32
            )
            spread(i, columns, terms.astype(BF16), outs)


def grad_call(parts, active, slope, gate_w, up_w, down_w):
    units, width = gate_w.shape
    count = parts[0].shape[0]
    total = SIDE * count
    return kernel_call(
        grad_body,
        (shape_of(total, units), shape_of(total, units)) + term_shapes(count, width),
        [pl.ANY] * 5 + [pltpu.VMEM] * 2 + [pl.ANY] * 3,
        [
            pltpu.VMEM((total, width), BF16),
            pltpu.VMEM((units, width), BF16),
            pltpu.VMEM((units, width), BF16),
            pltpu.VMEM((units, width), BF16),
            pltpu.SemaphoreType.DMA((8,)),
        ],
        *parts, active, slope, gate_w, up_w, down_w,
    )


def sums_body(*refs):
    stash, grads, (gate_act, up_act, hidden, order) = refs[:5], refs[5:10], refs[10:14]
    (keep, send), (stash_v, grad_v, sems) = refs[14:16], refs[16:]
    copies = started(stash, pieces_of(stash_v), sems) + started(grads, pieces_of(grad_v), sems, 5)
    units, size = gate_act.shape[1], keep.shape[2]
    for copy in copies:
        copy.wait()
    lefts = ((gate_act[...], stash_v), (up_act[...], stash_v), (hidden[...], grad_v))
    for i, out in ((1, send), (0, keep)):
        for j in range(2):
            columns = pl.ds(pl.multiple_of(order[2 * i + j] * size, 128), size)
            for k, (lhs, rhs) in enumerate(lefts):
                out[j, pl.ds(k * units, units), :] = lax.dot_general(
                    lhs, rhs[:, columns], CONTRACT_FIRST, preferred_element_type=F32
                ).astype(BF16)


def sums_call(stash, grads, gate_act, up_act, hidden, order):
    total, units = gate_act.shape
    width = stash[0].shape[1]
    out = shape_of(2, 3 * units, width // 4)
    return kernel_call(
        sums_body,
        (out, out),
        [pl.ANY] * 10 + [pltpu.VMEM] * 3 + [pltpu.SMEM],
        [
            pltpu.VMEM((total, width), BF16),
            pltpu.VMEM((total, width), BF16),
            pltpu.SemaphoreType.DMA((10,)),
        ],
        *stash, *grads, gate_act, up_act, hidden, order,
    )


def fwd_body(*refs):
    parts, (gate, up, down), outs = refs[:5], refs[5:8], refs[8:13]
    rows, gate_v, up_v, down_v, sems = refs[13:]
    weights = started((gate, up), (gate_v, up_v), sems)
    copies = started(parts, pieces_of(rows), sems, 2)
    later = started((down,), (down_v,), sems, 7)
    for copy in weights:
        copy.wait()
    half, width = rows.shape[0] // 2, rows.shape[1]
    step = width // SIDE
    for i, needed in enumerate((copies[:2], copies[2:])):
        for copy in needed:
            copy.wait()
        _, pre_up, _, act = gate_and_up(rows[pl.ds(i * half, half), :], gate_v[...], up_v[...])
        hidden = (act * pre_up).astype(BF16)
        if i == 0:
            later[0].wait()
        for j in range(SIDE):
            columns = pl.ds(j * step, step)
            terms = jnp.dot(hidden, down_v[:, columns], preferred_element_type=F32)
            spread(i, columns, terms.astype(BF16), outs)


def fwd_call(parts, gate_w, up_w, down_w):
    units, width = gate_w.shape
    count = parts[0].shape[0]
    return kernel_call(
        fwd_body,
        term_shapes(count, width),
        [pl.ANY] * 8,
        [
            pltpu.VMEM((SIDE * count, width), BF16),
            pltpu.VMEM((units, width), BF16),
            pltpu.VMEM((units, width), BF16),
            pltpu.VMEM((units, width), BF16),
            pltpu.SemaphoreType.DMA((8,)),
        ],
        *parts, gate_w, up_w, down_w,
    )


def per_device(
    handoff,
    fwd_slot,
    fwd_weight,
    stashed,
    back_slot,
    back_weight,
    grad_handoff,
    w_gate,
    w_up,
    w_down,
):
    gate_w, up_w, down_w = (w_gate[0].T, w_up[0].T, w_down[0])
    fwd_ids = fwd_slot[0]
    back_ids = back_slot[0]
    place = lax.axis_index("dp")
    core, z_lo = place % 2, place // 2

    returned = passed_along(grad_handoff, "section", -1)[0]
    arrived = passed_along(handoff, "section", 1)[0]

    stash_own = pack_rows(stashed[0], back_ids)
    stash_rows = z_ordered(stash_own, fetched_z(stash_own))
    stash_near = y_first(stash_rows)
    returned = tied(returned, stash_rows)
    scaled = (back_weight[0][:, None] * returned.astype(F32)).astype(BF16)
    grad_own = pack_rows(scaled, back_ids)
    grad_rows = z_ordered(grad_own, fetched_z(tied(grad_own, stash_rows)))
    grad_near = y_first(tied(grad_rows, *stash_near))
    fwd_own = pack_rows(tied(arrived, grad_own), fwd_ids)
    stash_far = y_second(*stash_near)
    fwd_rows = gathered_z(tied(fwd_own, grad_rows, *stash_far))
    back_all = pieces(tied(stash_rows, grad_rows), stash_near, stash_far)
    hidden, active, slope = act_call(back_all, gate_w, up_w)
    grad_far = y_second(*(tied(t, hidden) for t in grad_near))
    fwd_near = y_first(tied(fwd_rows, *grad_far))
    grad_all = pieces(tied(grad_rows, active, fwd_rows), grad_near, grad_far)
    gate_act, up_act, own, right, far_a, far_b, left = grad_call(
        grad_all, active, slope, gate_w, up_w, down_w
    )
    input_far = far_out(far_a, far_b)
    fwd_far = y_second(*(tied(t, far_a) for t in fwd_near))
    order = jnp.stack(
        [(z_lo ^ i) * 2 + (core ^ j) for j in range(2) for i in range(2)]
    ).astype(jnp.int32)
    keep, send = sums_call(
        back_all, grad_all, gate_act, up_act, hidden, order
    )
    came = swapped(tied(send, *fwd_near, *input_far), 1)
    give = added(keep[1], came[1])
    input_near = near_out(right, left, tuple(tied(t, give, *fwd_far) for t in input_far))
    gave = swapped(give, 2)
    fwd_terms = fwd_call(
        pieces(tied(fwd_rows, give), fwd_near, fwd_far), gate_w, up_w, down_w
    )
    fwd_out_far = far_out(fwd_terms[2], fwd_terms[3])
    input_terms = added(own, *input_near)
    width = own.shape[1] // 2
    fwd_out_far = tuple(tied(t, input_terms, gave) for t in fwd_out_far)
    halves = []
    for columns in (slice(0, width), slice(width, None)):
        near = near_out(
            fwd_terms[1][:, columns],
            fwd_terms[4][:, columns],
            tuple(t[:, columns] for t in fwd_out_far),
        )
        halves.append(added(fwd_terms[0][:, columns], *near))
    input_came = exchanged_z(input_terms)
    fwd_z = halves[1]
    input_sum = sum(part.astype(F32) for part in split(tied(input_came, fwd_z)))
    input_grad = unpack_rows(input_sum, back_ids).astype(BF16)
    sums = added(tied(keep[0], fwd_z), came[0], gave)
    third = sums.shape[0] // 3
    gate_sum, up_sum, down_sum = sums[:third].T, sums[third : 2 * third].T, sums[2 * third :]
    fwd_sum = jnp.concatenate([total_of(*sent_z(half)) for half in halves], axis=1)
    forward_out = (fwd_weight[0][:, None] * unpack_rows(fwd_sum, fwd_ids)).astype(BF16)
    return (forward_out[None], input_grad[None], gate_sum[None], up_sum[None], down_sum[None])


def solution(mesh):
    placed = (
        P("section", ("dp", "et"), None),
        P("section", ("dp", "et")),
        P("section", ("dp", "et")),
        P("section", ("dp", "et"), None),
        P("section", ("dp", "et")),
        P("section", ("dp", "et")),
        P("section", ("dp", "et"), None),
        P("section", None, "et"),
        P("section", None, "et"),
        P("section", "et", None),
    )
    return jax.shard_map(
        per_device,
        mesh=mesh,
        in_specs=placed,
        out_specs=(
            P("section", ("dp", "et"), None),
            P("section", ("dp", "et"), None),
            P("section", "dp", "et"),
            P("section", "dp", "et"),
            P("section", "et", "dp"),
        ),
        check_vma=False,
    )
```
